32 devices in a mesh: ctx: 8 (over y, x, core), tp: 4 (over z).
Axes of the slice: x: 2, y: 2, z: 4, core: 2. Of those that a mesh axis runs over, the one named last changes fastest.
Arguments:
- query_act: bfloat16 [4096, 4096], P('ctx', 'tp'), may hold values from -6 to 6
- key_act: bfloat16 [4096, 4096], P('ctx', 'tp'), may hold values from -6 to 6
- value_act: bfloat16 [4096, 4096], P('ctx', 'tp'), may hold values from -6 to 6
- out_grad: bfloat16 [4096, 4096], P('ctx', 'tp'), may hold values from -6 to 6
- filters: float32 [256, 4096], P('tp', 'ctx'), may hold values from -6 to 6
Outputs:
- query_grad: bfloat16 [4096, 4096], P('ctx', 'tp')
- key_grad: bfloat16 [4096, 4096], P('ctx', 'tp')
- value_grad: bfloat16 [4096, 4096], P('ctx', 'tp')
- filter_grad: float32 [256, 4096], P('tp', 'ctx')
The draws below stay inside these ranges and needn't reach their ends.
All inputs are finite; a program needn't handle non-finite values.
Results may differ from the reference program's by a relative error of at most 0.006.
Values may be sent and summed in bfloat16 or wider, within the bound.
A program may use at most 128 MiB of HBM per device.

```python
import jax
import jax.numpy as jnp
from jax import lax

D = 4096
GROUP_CH = 16
GROUPS = 256
SEQ = 4096


def shard_levels(own_key, extent, shards, smallest, top_value):
    factor_of, own = 1.0, jax.random.fold_in(own_key, 6)
    for dim, shards_of in shards:
        steps = jnp.exp(jax.random.uniform(jax.random.fold_in(own, dim), (shards_of,), jnp.float32, smallest / len(shards), top_value / len(shards)))
        factor_of = factor_of * jnp.repeat(steps, extent[dim] // shards_of).reshape([-1 if axis == dim else 1 for axis in range(len(extent))])
    return factor_of


def normal_values(stream_key, extent, scale, most, split=(), kind=jnp.bfloat16):
    values = scale * jax.random.normal(stream_key, extent, jnp.float32)
    if split:
        values = values * shard_levels(stream_key, extent, split, -0.22, 0.18)
    return jnp.clip(values, -most, most).astype(kind)


def setup_inputs(seed: int = 0) -> dict:
    keys = jax.random.split(jax.random.key(seed), 6)
    query_act = normal_values(keys[0], (SEQ, D), 1.0, 6.0, ((0, 8), (1, 4)))
    key_act = normal_values(keys[1], (SEQ, D), 1.0, 6.0, ((0, 8), (1, 4)))
    value_act = normal_values(keys[2], (SEQ, D), 1.0, 6.0, ((0, 8), (1, 4)))
    out_grad = normal_values(keys[3], (SEQ, D), 1.0, 6.0, ((0, 8), (1, 4)))
    filters = normal_values(keys[4], (GROUPS, SEQ), 1.0, 6.0, ((0, 4), (1, 8)), jnp.float32)
    return {"query_act": query_act, "key_act": key_act, "value_act": value_act, "out_grad": out_grad, "filters": filters}


def group_terms(block):
    query_blk, key_blk, value_blk, grad_blk, filter_row = block
    full_len = 2 * SEQ
    filter_scale = 1.0 / (SEQ ** 0.5)
    kv_low = (key_blk.astype(jnp.float32) * value_blk.astype(jnp.float32)).astype(jnp.bfloat16)
    kv_low = lax.optimization_barrier(kv_low)
    kv_prod = kv_low.astype(jnp.float32)
    gated_low = (grad_blk.astype(jnp.float32) * query_blk.astype(jnp.float32)).astype(jnp.bfloat16)
    gated_low = lax.optimization_barrier(gated_low)
    gated = gated_low.astype(jnp.float32)
    filt_spec = jnp.fft.rfft(filter_row * filter_scale, n=full_len)
    kv_spec = jnp.fft.rfft(kv_prod, n=full_len, axis=0)
    gated_spec = jnp.fft.rfft(gated, n=full_len, axis=0)
    conv_out = jnp.fft.irfft(filt_spec[:, None] * kv_spec, n=full_len, axis=0)[:SEQ].astype(jnp.bfloat16)
    conv_grad = jnp.fft.irfft(jnp.conj(filt_spec)[:, None] * gated_spec, n=full_len, axis=0)[:SEQ].astype(jnp.bfloat16)
    cross = jnp.sum(jnp.conj(kv_spec) * gated_spec, axis=1)
    filter_grad = (jnp.fft.irfft(cross, n=full_len)[:SEQ] * filter_scale).astype(jnp.float32)
    query_grad = (grad_blk.astype(jnp.float32) * conv_out.astype(jnp.float32)).astype(jnp.bfloat16)
    key_grad = (conv_grad.astype(jnp.float32) * value_blk.astype(jnp.float32)).astype(jnp.bfloat16)
    value_grad = (conv_grad.astype(jnp.float32) * key_blk.astype(jnp.float32)).astype(jnp.bfloat16)
    return query_grad, key_grad, value_grad, filter_grad


def reference(query_act, key_act, value_act, out_grad, filters):
    groups = D // GROUP_CH

    def regroup(array):
        return array.reshape(SEQ, groups, GROUP_CH).transpose(1, 0, 2)

    def ungroup(array):
        return array.transpose(1, 0, 2).reshape(SEQ, D)

    results = lax.map(group_terms, (regroup(query_act), regroup(key_act), regroup(value_act), regroup(out_grad), filters))
    return ungroup(results[0]), ungroup(results[1]), ungroup(results[2]), results[3]
```

```python
import functools
import math

import jax
import jax.numpy as jnp
from jax import lax
from jax.experimental import pallas as pl
from jax.experimental.pallas import tpu as pltpu
from jax.sharding import PartitionSpec as P

GROUP_CH = 16


HIGH = lax.Precision.HIGHEST


def make_tables(outer_len, inner_len, full_len):
    half_rows = outer_len // 2
    freq_idx = lax.iota(jnp.int32, outer_len)[:, None]
    time_idx = lax.iota(jnp.int32, half_rows)[None, :]
    outer_angle = (freq_idx * time_idx % outer_len).astype(jnp.float32) * (
        2.0 * math.pi / outer_len
    )
    inner_idx = lax.iota(jnp.int32, inner_len)
    inner_angle = (inner_idx[:, None] * inner_idx[None, :] % inner_len).astype(jnp.float32) * (
        2.0 * math.pi / inner_len
    )
    inner_cos = jnp.cos(inner_angle)
    inner_sin = jnp.sin(inner_angle)
    forward_mat = jnp.concatenate(
        [jnp.concatenate([inner_cos, -inner_sin], 1), jnp.concatenate([inner_sin, inner_cos], 1)], 0
    )
    inverse_mat = jnp.concatenate(
        [jnp.concatenate([inner_cos, inner_sin], 1), jnp.concatenate([-inner_sin, inner_cos], 1)], 0
    )
    twist_angle = (freq_idx * inner_idx[None, :] % full_len).astype(jnp.float32) * (
        2.0 * math.pi / full_len
    )
    return (
        jnp.cos(outer_angle),
        jnp.sin(outer_angle),
        forward_mat,
        inverse_mat,
        jnp.cos(twist_angle),
        jnp.sin(twist_angle),
    )


def transform(signal, tables):
    outer_cos, outer_sin, forward_mat, inverse_mat, twist_cos, twist_sin = tables
    outer_len, half_rows = outer_cos.shape
    inner_len = twist_cos.shape[1]
    count = signal.shape[0]
    folded = signal.reshape(count, half_rows, inner_len)
    first_re = jnp.einsum("ka,cab->ckb", outer_cos, folded, precision=HIGH)
    first_im = -jnp.einsum("ka,cab->ckb", outer_sin, folded, precision=HIGH)
    turned_re = first_re * twist_cos + first_im * twist_sin
    turned_im = first_im * twist_cos - first_re * twist_sin
    joined = jnp.concatenate([turned_re, turned_im], -1).reshape(count * outer_len, 2 * inner_len)
    spectrum = jnp.dot(joined, forward_mat, precision=HIGH, preferred_element_type=jnp.float32)
    spectrum = spectrum.reshape(count, outer_len, 2 * inner_len)
    return (spectrum[..., :inner_len], spectrum[..., inner_len:])


def untransform(real_part, imag_part, tables):
    outer_cos, outer_sin, forward_mat, inverse_mat, twist_cos, twist_sin = tables
    outer_len, half_rows = outer_cos.shape
    inner_len = twist_cos.shape[1]
    count = real_part.shape[0]
    joined = jnp.concatenate([real_part, imag_part], -1).reshape(count * outer_len, 2 * inner_len)
    mixed = jnp.dot(joined, inverse_mat, precision=HIGH, preferred_element_type=jnp.float32)
    mixed = mixed.reshape(count, outer_len, 2 * inner_len)
    mixed_re = mixed[..., :inner_len]
    mixed_im = mixed[..., inner_len:]
    turned_re = mixed_re * twist_cos - mixed_im * twist_sin
    turned_im = mixed_re * twist_sin + mixed_im * twist_cos
    signal = jnp.einsum("ka,ckb->cab", outer_cos, turned_re, precision=HIGH) - jnp.einsum(
        "ka,ckb->cab", outer_sin, turned_im, precision=HIGH
    )
    return signal.reshape(count, half_rows * inner_len) / (2.0 * half_rows * inner_len)


def convolve(kv_prod, gated, spread, tables, filter_scale):
    channels = kv_prod.shape[0]
    groups_here = spread.shape[0]
    outer_len = tables[0].shape[0]
    inner_len = tables[4].shape[1]
    filt_re, filt_im = transform(spread, tables)
    filt_re = (filt_re * filter_scale)[:, None]
    filt_im = (filt_im * filter_scale)[:, None]
    both_re, both_im = transform(jnp.concatenate([kv_prod, gated], 0).astype(jnp.float32), tables)
    grouped = (groups_here, GROUP_CH, outer_len, inner_len)
    kv_re = both_re[:channels].reshape(grouped)
    kv_im = both_im[:channels].reshape(grouped)
    gated_re = both_re[channels:].reshape(grouped)
    gated_im = both_im[channels:].reshape(grouped)
    out_re = filt_re * kv_re - filt_im * kv_im
    out_im = filt_re * kv_im + filt_im * kv_re
    back_re = filt_re * gated_re + filt_im * gated_im
    back_im = filt_re * gated_im - filt_im * gated_re
    cross_re = jnp.sum(kv_re * gated_re + kv_im * gated_im, 1)
    cross_im = jnp.sum(kv_re * gated_im - kv_im * gated_re, 1)
    flat = (channels, outer_len, inner_len)
    stacked_re = jnp.concatenate([out_re.reshape(flat), back_re.reshape(flat), cross_re], 0)
    stacked_im = jnp.concatenate([out_im.reshape(flat), back_im.reshape(flat), cross_im], 0)
    signals = untransform(stacked_re, stacked_im, tables)
    conv_out = signals[:channels].astype(jnp.bfloat16)
    conv_grad = signals[channels : 2 * channels].astype(jnp.bfloat16)
    filt_grad = signals[2 * channels :] * filter_scale
    return (conv_out, conv_grad, filt_grad)


def product(first, second):
    return (first.astype(jnp.float32) * second.astype(jnp.float32)).astype(jnp.bfloat16)


def spectral_body(query_act, key_act, value_act, out_grad, filters):
    tokens = query_act.shape[0]
    ctx_size = lax.axis_size("ctx")
    seq_len = tokens * ctx_size
    full_len = 2 * seq_len
    inner_len = math.gcd(full_len, 1 << full_len.bit_length() // 2)
    outer_len = full_len // inner_len
    tables = make_tables(outer_len, inner_len, full_len)
    filter_scale = 1.0 / math.sqrt(seq_len)
    spread = lax.all_to_all(filters, "ctx", split_axis=0, concat_axis=1, tiled=True)
    kv_local = product(key_act, value_act).T
    gated_local = product(out_grad, query_act).T
    kv_prod, gated = (
        lax.all_to_all(kv_local, "ctx", split_axis=0, concat_axis=1, tiled=True),
        lax.all_to_all(gated_local, "ctx", split_axis=0, concat_axis=1, tiled=True),
    )
    conv_out, conv_grad, filt_grad = convolve(kv_prod, gated, spread, tables, filter_scale)
    filter_grad = lax.all_to_all(filt_grad, "ctx", split_axis=1, concat_axis=0, tiled=True)
    returned = (
        lax.all_to_all(conv_out, "ctx", split_axis=1, concat_axis=0, tiled=True),
        lax.all_to_all(conv_grad, "ctx", split_axis=1, concat_axis=0, tiled=True),
    )
    conv_local = returned[0].T
    grad_local = returned[1].T
    query_grad = product(out_grad, conv_local)
    key_grad = product(grad_local, value_act)
    value_grad = product(grad_local, key_act)
    return (query_grad, key_grad, value_grad, filter_grad)


LANES = 128
BLOCK = 2 * LANES
MAX_BLOCKS = 16
MESH = pl.DeviceIdType.MESH


def dot(left, right, contract):
    return lax.dot_general(left, right, (contract, ((), ())), preferred_element_type=jnp.float32)


def diagonal_sums(tile):
    rows = LANES
    while rows > 8:
        rows //= 2
        tile = tile[:rows] + pltpu.roll(tile[rows:], LANES - rows, 1)
    row = lax.broadcasted_iota(jnp.int32, tile.shape, 0)
    for step in (4, 2, 1):
        tile = jnp.where(row // step % 2 == 1, pltpu.roll(tile, LANES - step, 1), tile)
    return jnp.sum(tile, axis=0, keepdims=True)


def conv_kernel(
    n,
    scale,
    query_ref,
    key_ref,
    value_ref,
    grad_ref,
    filt_ref,
    ret_ref,
    fgrad_ref,
    outbox,
    inbox,
    results,
    taps,
    tap_grads,
    tap_rows,
    grad_rows,
    toeplitz,
    padded,
    conv_acc,
    back_acc,
    fwd_send,
    fwd_recv,
    ret_send,
    ret_recv,
    tap_send,
    tap_recv,
    fg_send,
    fg_recv,
    local_sems,
):
    me = lax.axis_index("ctx")
    tokens, chans = query_ref.shape
    parts = tokens // BLOCK
    rows_here = parts * GROUP_CH
    groups = inbox.shape[0]
    rows = inbox.shape[2]
    blocks = rows // GROUP_CH
    lanes_here = chans // n

    barrier = pltpu.get_barrier_semaphore()
    peers = [lax.rem(me + step, n) for step in range(1, n)]
    for peer in peers:
        pl.semaphore_signal(barrier, inc=1, device_id={"ctx": peer}, device_id_type=MESH)

    def fill(block, carry):
        lane = pl.ds(pl.multiple_of(block * LANES, LANES), LANES)
        first = block * (LANES // GROUP_CH)
        for part in range(parts):
            rows_of = pl.ds(part * BLOCK, BLOCK)
            for which, (one, two) in enumerate(((key_ref, value_ref), (grad_ref, query_ref))):
                prod = one[rows_of, lane].astype(jnp.float32) * two[rows_of, lane].astype(jnp.float32)
                turned = prod.astype(jnp.bfloat16).T
                outbox[pl.ds(first, LANES // GROUP_CH), which, pl.ds(part * GROUP_CH, GROUP_CH), :] = (
                    turned.reshape(LANES // GROUP_CH, GROUP_CH, BLOCK)
                )
        return carry

    lax.fori_loop(0, chans // LANES, fill, 0)

    def tap_copy(peer):
        return pltpu.make_async_remote_copy(
            src_ref=filt_ref.at[pl.ds(pl.multiple_of(peer * groups, groups), groups), :],
            dst_ref=taps.at[me],
            send_sem=tap_send.at[peer],
            recv_sem=tap_recv.at[me],
            device_id={"ctx": peer},
            device_id_type=MESH,
        )

    def fwd_copy(group, peer):
        return pltpu.make_async_remote_copy(
            src_ref=outbox.at[peer * groups + group],
            dst_ref=inbox.at[group, :, pl.ds(pl.multiple_of(me * rows_here, rows_here), rows_here), :],
            send_sem=fwd_send.at[group, peer],
            recv_sem=fwd_recv.at[group, me],
            device_id={"ctx": peer},
            device_id_type=MESH,
        )

    def fwd_arrival(group, peer):
        return pltpu.make_async_remote_copy(
            src_ref=outbox.at[peer * groups + group],
            dst_ref=inbox.at[group, :, pl.ds(pl.multiple_of(peer * rows_here, rows_here), rows_here), :],
            send_sem=fwd_send.at[group, peer],
            recv_sem=fwd_recv.at[group, peer],
            device_id={"ctx": peer},
            device_id_type=MESH,
        )

    def ret_copy(group, peer):
        return pltpu.make_async_remote_copy(
            src_ref=results.at[group, :, pl.ds(pl.multiple_of(peer * rows_here, rows_here), rows_here), :],
            dst_ref=ret_ref.at[me * groups + group],
            send_sem=ret_send.at[group, peer],
            recv_sem=ret_recv.at[group, me],
            device_id={"ctx": peer},
            device_id_type=MESH,
        )

    def ret_arrival(group, peer):
        return pltpu.make_async_remote_copy(
            src_ref=results.at[group, :, pl.ds(pl.multiple_of(peer * rows_here, rows_here), rows_here), :],
            dst_ref=ret_ref.at[peer * groups + group],
            send_sem=ret_send.at[group, peer],
            recv_sem=ret_recv.at[group, peer],
            device_id={"ctx": peer},
            device_id_type=MESH,
        )

    def fg_copy(peer):
        return pltpu.make_async_remote_copy(
            src_ref=tap_grads.at[peer],
            dst_ref=fgrad_ref.at[pl.ds(pl.multiple_of(me * groups, groups), groups), :],
            send_sem=fg_send.at[peer],
            recv_sem=fg_recv.at[me],
            device_id={"ctx": peer},
            device_id_type=MESH,
        )

    def fg_arrival(peer):
        return pltpu.make_async_remote_copy(
            src_ref=tap_grads.at[peer],
            dst_ref=fgrad_ref.at[pl.ds(pl.multiple_of(peer * groups, groups), groups), :],
            send_sem=fg_send.at[peer],
            recv_sem=fg_recv.at[peer],
            device_id={"ctx": peer},
            device_id_type=MESH,
        )

    def tap_arrival(peer):
        return pltpu.make_async_remote_copy(
            src_ref=filt_ref.at[pl.ds(pl.multiple_of(peer * groups, groups), groups), :],
            dst_ref=taps.at[peer],
            send_sem=tap_send.at[peer],
            recv_sem=tap_recv.at[peer],
            device_id={"ctx": peer},
            device_id_type=MESH,
        )

    pl.semaphore_wait(barrier, n - 1)
    for peer in peers:
        tap_copy(peer).start()

    def send_group(group, carry):
        for peer in peers:
            fwd_copy(group, peer).start()
        return carry

    lax.fori_loop(0, groups, send_group, 0)
    own_rows = pl.ds(pl.multiple_of(me * rows_here, rows_here), rows_here)
    own_groups = pl.ds(pl.multiple_of(me * groups, groups), groups)
    own_taps = pltpu.make_async_copy(filt_ref.at[own_groups, :], taps.at[me], local_sems.at[0])
    own_in = pltpu.make_async_copy(outbox.at[own_groups], inbox.at[:, :, own_rows, :], local_sems.at[1])
    own_taps.start()
    own_in.start()

    padded[pl.ds(rows, LANES), :] = jnp.zeros((LANES, BLOCK), jnp.bfloat16)
    toeplitz[pl.ds(LANES, LANES), pl.ds(0, LANES)] = jnp.zeros((LANES, LANES), jnp.bfloat16)
    own_taps.wait()
    own_in.wait()
    for peer in peers:
        tap_arrival(peer).wait_recv()

    tiles = rows * BLOCK // GROUP_CH // LANES
    per_dev = tiles // n
    for group in range(groups):
        for tile in range(tiles):
            tap_rows[group, pl.ds(tile, 1), :] = (
                taps[tile // per_dev, pl.ds(group, 1), pl.ds(tile % per_dev * LANES, LANES)] * scale
            )
    row_idx = lax.broadcasted_iota(jnp.int32, (LANES, LANES), 0)
    lane_idx = lax.broadcasted_iota(jnp.int32, (LANES, LANES), 1)
    upper = lane_idx >= row_idx

    def one_group(group, carry):
        before = jnp.zeros((LANES, LANES), jnp.float32)
        for tile in range(tiles):
            line = tap_rows[group, pl.ds(tile, 1), :]
            now = pltpu.roll(jnp.broadcast_to(line, (LANES, LANES)), 0, 1, stride=1, stride_axis=0)
            both = jnp.where(upper, now, before).astype(jnp.bfloat16)
            toeplitz[pl.ds(0, LANES), pl.ds(tile * LANES, LANES)] = both
            if tile + 1 < tiles:
                toeplitz[pl.ds(LANES, LANES), pl.ds((tile + 1) * LANES, LANES)] = both
            before = now
        for peer in peers:
            fwd_arrival(group, peer).wait_recv()
        padded[pl.ds(0, rows), :] = inbox[group, 1]
        turned = inbox[group, 0].T
        even_after = jnp.zeros((LANES, LANES), jnp.float32)
        carried = jnp.zeros((LANES, LANES), jnp.float32)
        conv_acc[...] = jnp.zeros(conv_acc.shape, jnp.float32)
        back_acc[...] = jnp.zeros(back_acc.shape, jnp.float32)
        for gap in reversed(range(blocks)):
            skip = gap * GROUP_CH
            count = rows - skip
            block_taps = toeplitz[:, pl.ds(gap * BLOCK, BLOCK)]
            conv_acc[pl.ds(skip, count), :] += dot(
                inbox[group, 0, pl.ds(0, count), :], block_taps, ((1,), (0,))
            )
            back_acc[pl.ds(0, count), :] += dot(
                padded[pl.ds(skip, count), :], block_taps, ((1,), (1,))
            )
            depth = -(-count // LANES) * LANES
            cross = dot(turned[:, :depth], padded[pl.ds(skip, depth), :], ((1,), (0,)))
            odd = cross[:LANES, LANES:] + carried
            even = cross[:LANES, :LANES] + cross[LANES:, LANES:]
            carried = cross[LANES:, :LANES]
            for tile, picked in (
                (2 * gap + 1, jnp.where(upper, odd, even_after)),
                (2 * gap, jnp.where(upper, even, odd)),
            ):
                grad_rows[group, pl.ds(tile, 1), :] = diagonal_sums(picked) * scale
            even_after = even
        results[group, 0] = conv_acc[...].astype(jnp.bfloat16)
        results[group, 1] = back_acc[...].astype(jnp.bfloat16)
        for peer in peers:
            ret_copy(group, peer).start()
        return carry

    lax.fori_loop(0, groups, one_group, 0)
    for group in range(groups):
        for tile in range(tiles):
            tap_grads[tile // per_dev, pl.ds(group, 1), pl.ds(tile % per_dev * LANES, LANES)] = (
                grad_rows[group, pl.ds(tile, 1), :]
            )
    for peer in peers:
        fg_copy(peer).start()
    own_ret = pltpu.make_async_copy(results.at[:, :, own_rows, :], ret_ref.at[own_groups], local_sems.at[2])
    own_fg = pltpu.make_async_copy(tap_grads.at[me], fgrad_ref.at[own_groups, :], local_sems.at[3])
    own_ret.start()
    own_fg.start()

    def finish_group(group, carry):
        for peer in peers:
            fwd_copy(group, peer).wait_send()
            ret_copy(group, peer).wait_send()
            ret_arrival(group, peer).wait_recv()
        return carry

    lax.fori_loop(0, groups, finish_group, 0)
    for peer in peers:
        tap_copy(peer).wait_send()
        fg_copy(peer).wait_send()
        fg_arrival(peer).wait_recv()
    own_ret.wait()
    own_fg.wait()


def finish_kernel(key_ref, value_ref, grad_ref, ret_ref, query_out, key_out, value_out):
    parts = key_ref.shape[0] // BLOCK
    for part in range(parts):
        rows_of = pl.ds(part * BLOCK, BLOCK)
        turned = []
        for which in range(2):
            piece = ret_ref[:, which, pl.ds(part * GROUP_CH, GROUP_CH), :]
            turned.append(piece.reshape(LANES, BLOCK).T.astype(jnp.float32))
        conv, back = turned
        query_out[rows_of, :] = (grad_ref[rows_of, :].astype(jnp.float32) * conv).astype(jnp.bfloat16)
        key_out[rows_of, :] = (back * value_ref[rows_of, :].astype(jnp.float32)).astype(jnp.bfloat16)
        value_out[rows_of, :] = (back * key_ref[rows_of, :].astype(jnp.float32)).astype(jnp.bfloat16)


def direct_body(query_act, key_act, value_act, out_grad, filters):
    tokens, chans = query_act.shape
    n = lax.axis_size("ctx")
    all_groups, taps_here = filters.shape
    groups = all_groups // n
    seq_len = tokens * n
    blocks = seq_len // BLOCK
    rows = blocks * GROUP_CH
    rows_here = rows // n
    vmem = pl.BlockSpec(memory_space=pltpu.VMEM)
    anywhere = pl.BlockSpec(memory_space=pl.ANY)
    dma = pltpu.SemaphoreType.DMA
    macs = groups * 3 * (rows + GROUP_CH) // 2 * blocks * BLOCK * BLOCK
    returned, fgrad = pl.pallas_call(
        functools.partial(conv_kernel, n, 1.0 / math.sqrt(seq_len)),
        out_shape=(
            jax.ShapeDtypeStruct((all_groups, 2, rows_here, BLOCK), jnp.bfloat16),
            jax.ShapeDtypeStruct((all_groups, taps_here), jnp.float32),
        ),
        in_specs=[vmem] * 5,
        out_specs=(anywhere, anywhere),
        scratch_shapes=[
            pltpu.VMEM((all_groups, 2, rows_here, BLOCK), jnp.bfloat16),
            pltpu.VMEM((groups, 2, rows, BLOCK), jnp.bfloat16),
            pltpu.VMEM((groups, 2, rows, BLOCK), jnp.bfloat16),
            pltpu.VMEM((n, groups, taps_here), jnp.float32),
            pltpu.VMEM((n, groups, taps_here), jnp.float32),
            pltpu.VMEM((groups, seq_len // LANES, LANES), jnp.float32),
            pltpu.VMEM((groups, seq_len // LANES, LANES), jnp.float32),
            pltpu.VMEM((BLOCK, seq_len), jnp.bfloat16),
            pltpu.VMEM((rows + LANES, BLOCK), jnp.bfloat16),
            pltpu.VMEM((rows, BLOCK), jnp.float32),
            pltpu.VMEM((rows, BLOCK), jnp.float32),
            dma((groups, n)),
            dma((groups, n)),
            dma((groups, n)),
            dma((groups, n)),
            dma((n,)),
            dma((n,)),
            dma((n,)),
            dma((n,)),
            dma((4,)),
        ],
        compiler_params=pltpu.CompilerParams(
            collective_id=0, has_side_effects=True, vmem_limit_bytes=48 * 1024 * 1024
        ),
        cost_estimate=pl.CostEstimate(flops=2 * macs, bytes_accessed=16 * tokens * chans, transcendentals=0),
    )(query_act, key_act, value_act, out_grad, filters)
    strip = pl.BlockSpec((tokens, LANES), lambda i: (0, i))
    side = jax.ShapeDtypeStruct((tokens, chans), jnp.bfloat16)
    query_grad, key_grad, value_grad = pl.pallas_call(
        finish_kernel,
        grid=(chans // LANES,),
        out_shape=(side, side, side),
        in_specs=[
            strip,
            strip,
            strip,
            pl.BlockSpec((LANES // GROUP_CH, 2, rows_here, BLOCK), lambda i: (i, 0, 0, 0)),
        ],
        out_specs=(strip, strip, strip),
        compiler_params=pltpu.CompilerParams(vmem_limit_bytes=32 * 1024 * 1024),
        cost_estimate=pl.CostEstimate(
            flops=3 * tokens * chans, bytes_accessed=16 * tokens * chans, transcendentals=0
        ),
    )(key_act, value_act, out_grad, returned)
    return (query_grad, key_grad, value_grad, fgrad)


def body(query_act, key_act, value_act, out_grad, filters):
    tokens, chans = query_act.shape
    n = lax.axis_size("ctx")
    groups = filters.shape[0] // n
    fits = (
        tokens % BLOCK == 0
        and chans % LANES == 0
        and filters.shape[1] % LANES == 0
        and groups % 8 == 0
        and tokens * n // BLOCK <= MAX_BLOCKS
    )
    if fits:
        return direct_body(query_act, key_act, value_act, out_grad, filters)
    return spectral_body(query_act, key_act, value_act, out_grad, filters)


def solution(mesh):
    return jax.shard_map(
        body,
        mesh=mesh,
        in_specs=(P("ctx", "tp"), P("ctx", "tp"), P("ctx", "tp"), P("ctx", "tp"), P("tp", "ctx")),
        out_specs=(P("ctx", "tp"), P("ctx", "tp"), P("ctx", "tp"), P("tp", "ctx")),
        check_vma=False,
    )
```

```python
import functools
import math

import jax
import jax.numpy as jnp
from jax import lax
from jax.experimental import pallas as pl
from jax.experimental.pallas import tpu as pltpu
from jax.sharding import PartitionSpec as P

GROUP_CH = 16


HIGH = lax.Precision.HIGHEST


def make_tables(outer_len, inner_len, full_len):
    half_rows = outer_len // 2
    freq_idx = lax.iota(jnp.int32, outer_len)[:, None]
    time_idx = lax.iota(jnp.int32, half_rows)[None, :]
    outer_angle = (freq_idx * time_idx % outer_len).astype(jnp.float32) * (
        2.0 * math.pi / outer_len
    )
    inner_idx = lax.iota(jnp.int32, inner_len)
    inner_angle = (inner_idx[:, None] * inner_idx[None, :] % inner_len).astype(jnp.float32) * (
        2.0 * math.pi / inner_len
    )
    inner_cos = jnp.cos(inner_angle)
    inner_sin = jnp.sin(inner_angle)
    forward_mat = jnp.concatenate(
        [jnp.concatenate([inner_cos, -inner_sin], 1), jnp.concatenate([inner_sin, inner_cos], 1)], 0
    )
    inverse_mat = jnp.concatenate(
        [jnp.concatenate([inner_cos, inner_sin], 1), jnp.concatenate([-inner_sin, inner_cos], 1)], 0
    )
    twist_angle = (freq_idx * inner_idx[None, :] % full_len).astype(jnp.float32) * (
        2.0 * math.pi / full_len
    )
    return (
        jnp.cos(outer_angle),
        jnp.sin(outer_angle),
        forward_mat,
        inverse_mat,
        jnp.cos(twist_angle),
        jnp.sin(twist_angle),
    )


def transform(signal, tables):
    outer_cos, outer_sin, forward_mat, inverse_mat, twist_cos, twist_sin = tables
    outer_len, half_rows = outer_cos.shape
    inner_len = twist_cos.shape[1]
    count = signal.shape[0]
    folded = signal.reshape(count, half_rows, inner_len)
    first_re = jnp.einsum("ka,cab->ckb", outer_cos, folded, precision=HIGH)
    first_im = -jnp.einsum("ka,cab->ckb", outer_sin, folded, precision=HIGH)
    turned_re = first_re * twist_cos + first_im * twist_sin
    turned_im = first_im * twist_cos - first_re * twist_sin
    joined = jnp.concatenate([turned_re, turned_im], -1).reshape(count * outer_len, 2 * inner_len)
    spectrum = jnp.dot(joined, forward_mat, precision=HIGH, preferred_element_type=jnp.float32)
    spectrum = spectrum.reshape(count, outer_len, 2 * inner_len)
    return (spectrum[..., :inner_len], spectrum[..., inner_len:])


def untransform(real_part, imag_part, tables):
    outer_cos, outer_sin, forward_mat, inverse_mat, twist_cos, twist_sin = tables
    outer_len, half_rows = outer_cos.shape
    inner_len = twist_cos.shape[1]
    count = real_part.shape[0]
    joined = jnp.concatenate([real_part, imag_part], -1).reshape(count * outer_len, 2 * inner_len)
    mixed = jnp.dot(joined, inverse_mat, precision=HIGH, preferred_element_type=jnp.float32)
    mixed = mixed.reshape(count, outer_len, 2 * inner_len)
    mixed_re = mixed[..., :inner_len]
    mixed_im = mixed[..., inner_len:]
    turned_re = mixed_re * twist_cos - mixed_im * twist_sin
    turned_im = mixed_re * twist_sin + mixed_im * twist_cos
    signal = jnp.einsum("ka,ckb->cab", outer_cos, turned_re, precision=HIGH) - jnp.einsum(
        "ka,ckb->cab", outer_sin, turned_im, precision=HIGH
    )
    return signal.reshape(count, half_rows * inner_len) / (2.0 * half_rows * inner_len)


def convolve(kv_prod, gated, spread, tables, filter_scale):
    channels = kv_prod.shape[0]
    groups_here = spread.shape[0]
    outer_len = tables[0].shape[0]
    inner_len = tables[4].shape[1]
    filt_re, filt_im = transform(spread, tables)
    filt_re = (filt_re * filter_scale)[:, None]
    filt_im = (filt_im * filter_scale)[:, None]
    both_re, both_im = transform(jnp.concatenate([kv_prod, gated], 0).astype(jnp.float32), tables)
    grouped = (groups_here, GROUP_CH, outer_len, inner_len)
    kv_re = both_re[:channels].reshape(grouped)
    kv_im = both_im[:channels].reshape(grouped)
    gated_re = both_re[channels:].reshape(grouped)
    gated_im = both_im[channels:].reshape(grouped)
    out_re = filt_re * kv_re - filt_im * kv_im
    out_im = filt_re * kv_im + filt_im * kv_re
    back_re = filt_re * gated_re + filt_im * gated_im
    back_im = filt_re * gated_im - filt_im * gated_re
    cross_re = jnp.sum(kv_re * gated_re + kv_im * gated_im, 1)
    cross_im = jnp.sum(kv_re * gated_im - kv_im * gated_re, 1)
    flat = (channels, outer_len, inner_len)
    stacked_re = jnp.concatenate([out_re.reshape(flat), back_re.reshape(flat), cross_re], 0)
    stacked_im = jnp.concatenate([out_im.reshape(flat), back_im.reshape(flat), cross_im], 0)
    signals = untransform(stacked_re, stacked_im, tables)
    conv_out = signals[:channels].astype(jnp.bfloat16)
    conv_grad = signals[channels : 2 * channels].astype(jnp.bfloat16)
    filt_grad = signals[2 * channels :] * filter_scale
    return (conv_out, conv_grad, filt_grad)


def product(first, second):
    return (first.astype(jnp.float32) * second.astype(jnp.float32)).astype(jnp.bfloat16)


def spectral_body(query_act, key_act, value_act, out_grad, filters):
    tokens = query_act.shape[0]
    ctx_size = lax.axis_size("ctx")
    seq_len = tokens * ctx_size
    full_len = 2 * seq_len
    inner_len = math.gcd(full_len, 1 << full_len.bit_length() // 2)
    outer_len = full_len // inner_len
    tables = make_tables(outer_len, inner_len, full_len)
    filter_scale = 1.0 / math.sqrt(seq_len)
    spread = lax.all_to_all(filters, "ctx", split_axis=0, concat_axis=1, tiled=True)
    kv_local = product(key_act, value_act).T
    gated_local = product(out_grad, query_act).T
    kv_prod, gated = (
        lax.all_to_all(kv_local, "ctx", split_axis=0, concat_axis=1, tiled=True),
        lax.all_to_all(gated_local, "ctx", split_axis=0, concat_axis=1, tiled=True),
    )
    conv_out, conv_grad, filt_grad = convolve(kv_prod, gated, spread, tables, filter_scale)
    filter_grad = lax.all_to_all(filt_grad, "ctx", split_axis=1, concat_axis=0, tiled=True)
    returned = (
        lax.all_to_all(conv_out, "ctx", split_axis=1, concat_axis=0, tiled=True),
        lax.all_to_all(conv_grad, "ctx", split_axis=1, concat_axis=0, tiled=True),
    )
    conv_local = returned[0].T
    grad_local = returned[1].T
    query_grad = product(out_grad, conv_local)
    key_grad = product(grad_local, value_act)
    value_grad = product(grad_local, key_act)
    return (query_grad, key_grad, value_grad, filter_grad)


LANES = 128
BLOCK = 2 * LANES
MAX_BLOCKS = 16
EARLY = 2
MESH = pl.DeviceIdType.MESH


def dot(left, right, contract):
    return lax.dot_general(left, right, (contract, ((), ())), preferred_element_type=jnp.float32)


def diagonal_sums(tile):
    rows = LANES
    while rows > 8:
        rows //= 2
        tile = tile[:rows] + pltpu.roll(tile[rows:], LANES - rows, 1)
    row = lax.broadcasted_iota(jnp.int32, tile.shape, 0)
    for step in (4, 2, 1):
        tile = jnp.where(row // step % 2 == 1, pltpu.roll(tile, LANES - step, 1), tile)
    return jnp.sum(tile, axis=0, keepdims=True)


def conv_kernel(
    n,
    scale,
    query_ref,
    key_ref,
    value_ref,
    grad_ref,
    filt_ref,
    ret_ref,
    fgrad_ref,
    held,
    outbox,
    inbox,
    results,
    taps,
    tap_grads,
    tap_rows,
    grad_rows,
    toeplitz,
    padded,
    conv_acc,
    back_acc,
    fwd_send,
    fwd_recv,
    ret_send,
    ret_recv,
    tap_send,
    tap_recv,
    fg_send,
    fg_recv,
    local_sems,
    load_sems,
):
    me = lax.axis_index("ctx")
    tokens, chans = query_ref.shape
    parts = tokens // BLOCK
    rows_here = parts * GROUP_CH
    groups = inbox.shape[0]
    rows = inbox.shape[2]
    blocks = rows // GROUP_CH
    lanes_here = chans // n

    barrier = pltpu.get_barrier_semaphore()
    peers = [lax.rem(me + step, n) for step in range(1, n)]
    for peer in peers:
        pl.semaphore_signal(barrier, inc=1, device_id={"ctx": peer}, device_id_type=MESH)

    arrays = (key_ref, value_ref, grad_ref, query_ref)

    def load(which, dest):
        strip = pl.ds(pl.multiple_of(dest * lanes_here, lanes_here), lanes_here)
        return pltpu.make_async_copy(
            arrays[which].at[:, strip], held.at[which, dest], load_sems.at[which, dest]
        )

    for step in range(1, n + 1):
        for which in range(4):
            load(which, lax.rem(me + step, n)).start()

    def fill(dest):
        for which in range(4):
            load(which, dest).wait()
        for strip in range(lanes_here // LANES):
            lane = pl.ds(strip * LANES, LANES)
            first = dest * groups + strip * (LANES // GROUP_CH)
            for part in range(parts):
                rows_of = pl.ds(part * BLOCK, BLOCK)
                for which in range(2):
                    one = held[2 * which, dest, rows_of, lane].astype(jnp.float32)
                    two = held[2 * which + 1, dest, rows_of, lane].astype(jnp.float32)
                    turned = (one * two).astype(jnp.bfloat16).T
                    outbox[
                        pl.ds(first, LANES // GROUP_CH), which, pl.ds(part * GROUP_CH, GROUP_CH), :
                    ] = turned.reshape(LANES // GROUP_CH, GROUP_CH, BLOCK)

    def tap_copy(peer):
        return pltpu.make_async_remote_copy(
            src_ref=filt_ref.at[pl.ds(pl.multiple_of(peer * groups, groups), groups), :],
            dst_ref=taps.at[me],
            send_sem=tap_send.at[peer],
            recv_sem=tap_recv.at[me],
            device_id={"ctx": peer},
            device_id_type=MESH,
        )

    def fwd_copy(group, peer):
        return pltpu.make_async_remote_copy(
            src_ref=outbox.at[peer * groups + group],
            dst_ref=inbox.at[group, :, pl.ds(pl.multiple_of(me * rows_here, rows_here), rows_here), :],
            send_sem=fwd_send.at[group, peer],
            recv_sem=fwd_recv.at[group, me],
            device_id={"ctx": peer},
            device_id_type=MESH,
        )

    def fwd_arrival(group, peer):
        return pltpu.make_async_remote_copy(
            src_ref=outbox.at[peer * groups + group],
            dst_ref=inbox.at[group, :, pl.ds(pl.multiple_of(peer * rows_here, rows_here), rows_here), :],
            send_sem=fwd_send.at[group, peer],
            recv_sem=fwd_recv.at[group, peer],
            device_id={"ctx": peer},
            device_id_type=MESH,
        )

    def ret_copy(group, peer):
        return pltpu.make_async_remote_copy(
            src_ref=results.at[group, :, pl.ds(pl.multiple_of(peer * rows_here, rows_here), rows_here), :],
            dst_ref=ret_ref.at[me * groups + group],
            send_sem=ret_send.at[group, peer],
            recv_sem=ret_recv.at[group, me],
            device_id={"ctx": peer},
            device_id_type=MESH,
        )

    def ret_arrival(group, peer):
        return pltpu.make_async_remote_copy(
            src_ref=results.at[group, :, pl.ds(pl.multiple_of(peer * rows_here, rows_here), rows_here), :],
            dst_ref=ret_ref.at[peer * groups + group],
            send_sem=ret_send.at[group, peer],
            recv_sem=ret_recv.at[group, peer],
            device_id={"ctx": peer},
            device_id_type=MESH,
        )

    def fg_copy(peer):
        return pltpu.make_async_remote_copy(
            src_ref=tap_grads.at[peer],
            dst_ref=fgrad_ref.at[pl.ds(pl.multiple_of(me * groups, groups), groups), :],
            send_sem=fg_send.at[peer],
            recv_sem=fg_recv.at[me],
            device_id={"ctx": peer},
            device_id_type=MESH,
        )

    def fg_arrival(peer):
        return pltpu.make_async_remote_copy(
            src_ref=tap_grads.at[peer],
            dst_ref=fgrad_ref.at[pl.ds(pl.multiple_of(peer * groups, groups), groups), :],
            send_sem=fg_send.at[peer],
            recv_sem=fg_recv.at[peer],
            device_id={"ctx": peer},
            device_id_type=MESH,
        )

    def tap_arrival(peer):
        return pltpu.make_async_remote_copy(
            src_ref=filt_ref.at[pl.ds(pl.multiple_of(peer * groups, groups), groups), :],
            dst_ref=taps.at[peer],
            send_sem=tap_send.at[peer],
            recv_sem=tap_recv.at[peer],
            device_id={"ctx": peer},
            device_id_type=MESH,
        )

    pl.semaphore_wait(barrier, n - 1)
    for peer in peers:
        tap_copy(peer).start()

    def fill_and_send(step, carry):
        dest = lax.rem(me + step, n)
        fill(dest)
        for group in range(EARLY):
            fwd_copy(group, dest).start()
        return carry

    lax.fori_loop(1, n, fill_and_send, 0)

    def send_group(group, carry):
        for peer in peers:
            fwd_copy(group, peer).start()
        return carry

    lax.fori_loop(EARLY, groups, send_group, 0)
    fill(me)
    own_rows = pl.ds(pl.multiple_of(me * rows_here, rows_here), rows_here)
    own_groups = pl.ds(pl.multiple_of(me * groups, groups), groups)
    own_taps = pltpu.make_async_copy(filt_ref.at[own_groups, :], taps.at[me], local_sems.at[0])
    own_in = pltpu.make_async_copy(outbox.at[own_groups], inbox.at[:, :, own_rows, :], local_sems.at[1])
    own_taps.start()
    own_in.start()

    padded[pl.ds(rows, LANES), :] = jnp.zeros((LANES, BLOCK), jnp.bfloat16)
    toeplitz[pl.ds(LANES, LANES), pl.ds(0, LANES)] = jnp.zeros((LANES, LANES), jnp.bfloat16)
    own_taps.wait()
    own_in.wait()
    for peer in peers:
        tap_arrival(peer).wait_recv()

    tiles = rows * BLOCK // GROUP_CH // LANES
    per_dev = tiles // n
    for group in range(groups):
        for tile in range(tiles):
            tap_rows[group, pl.ds(tile, 1), :] = (
                taps[tile // per_dev, pl.ds(group, 1), pl.ds(tile % per_dev * LANES, LANES)] * scale
            )
    row_idx = lax.broadcasted_iota(jnp.int32, (LANES, LANES), 0)
    lane_idx = lax.broadcasted_iota(jnp.int32, (LANES, LANES), 1)
    upper = lane_idx >= row_idx

    def one_group(group, carry):
        before = jnp.zeros((LANES, LANES), jnp.float32)
        for tile in range(tiles):
            line = tap_rows[group, pl.ds(tile, 1), :]
            now = pltpu.roll(jnp.broadcast_to(line, (LANES, LANES)), 0, 1, stride=1, stride_axis=0)
            both = jnp.where(upper, now, before).astype(jnp.bfloat16)
            toeplitz[pl.ds(0, LANES), pl.ds(tile * LANES, LANES)] = both
            if tile + 1 < tiles:
                toeplitz[pl.ds(LANES, LANES), pl.ds((tile + 1) * LANES, LANES)] = both
            before = now
        for peer in peers:
            fwd_arrival(group, peer).wait_recv()
        padded[pl.ds(0, rows), :] = inbox[group, 1]
        turned = inbox[group, 0].T
        even_after = jnp.zeros((LANES, LANES), jnp.float32)
        carried = jnp.zeros((LANES, LANES), jnp.float32)
        conv_acc[...] = jnp.zeros(conv_acc.shape, jnp.float32)
        back_acc[...] = jnp.zeros(back_acc.shape, jnp.float32)
        for gap in reversed(range(blocks)):
            skip = gap * GROUP_CH
            count = rows - skip
            block_taps = toeplitz[:, pl.ds(gap * BLOCK, BLOCK)]
            conv_acc[pl.ds(skip, count), :] += dot(
                inbox[group, 0, pl.ds(0, count), :], block_taps, ((1,), (0,))
            )
            back_acc[pl.ds(0, count), :] += dot(
                padded[pl.ds(skip, count), :], block_taps, ((1,), (1,))
            )
            depth = -(-count // LANES) * LANES
            cross = dot(turned[:, :depth], padded[pl.ds(skip, depth), :], ((1,), (0,)))
            odd = cross[:LANES, LANES:] + carried
            even = cross[:LANES, :LANES] + cross[LANES:, LANES:]
            carried = cross[LANES:, :LANES]
            for tile, picked in (
                (2 * gap + 1, jnp.where(upper, odd, even_after)),
                (2 * gap, jnp.where(upper, even, odd)),
            ):
                grad_rows[group, pl.ds(tile, 1), :] = diagonal_sums(picked) * scale
            even_after = even
        results[group, 0] = conv_acc[...].astype(jnp.bfloat16)
        results[group, 1] = back_acc[...].astype(jnp.bfloat16)
        for peer in peers:
            ret_copy(group, peer).start()
        return carry

    lax.fori_loop(0, groups, one_group, 0)
    for group in range(groups):
        for tile in range(tiles):
            tap_grads[tile // per_dev, pl.ds(group, 1), pl.ds(tile % per_dev * LANES, LANES)] = (
                grad_rows[group, pl.ds(tile, 1), :]
            )
    for peer in peers:
        fg_copy(peer).start()
    own_ret = pltpu.make_async_copy(results.at[:, :, own_rows, :], ret_ref.at[own_groups], local_sems.at[2])
    own_fg = pltpu.make_async_copy(tap_grads.at[me], fgrad_ref.at[own_groups, :], local_sems.at[3])
    own_ret.start()
    own_fg.start()

    def finish_group(group, carry):
        for peer in peers:
            fwd_copy(group, peer).wait_send()
            ret_copy(group, peer).wait_send()
            ret_arrival(group, peer).wait_recv()
        return carry

    lax.fori_loop(0, groups, finish_group, 0)
    for peer in peers:
        tap_copy(peer).wait_send()
        fg_copy(peer).wait_send()
        fg_arrival(peer).wait_recv()
    own_ret.wait()
    own_fg.wait()


def finish_kernel(
    key_ref, value_ref, grad_ref, ret_ref, fgrad_ref, query_out, key_out, value_out, fgrad_out
):
    fgrad_out[...] = fgrad_ref[...]
    parts = key_ref.shape[0] // BLOCK
    for part in range(parts):
        rows_of = pl.ds(part * BLOCK, BLOCK)
        turned = []
        for which in range(2):
            piece = ret_ref[:, which, pl.ds(part * GROUP_CH, GROUP_CH), :]
            turned.append(piece.reshape(LANES, BLOCK).T.astype(jnp.float32))
        conv, back = turned
        query_out[rows_of, :] = (grad_ref[rows_of, :].astype(jnp.float32) * conv).astype(jnp.bfloat16)
        key_out[rows_of, :] = (back * value_ref[rows_of, :].astype(jnp.float32)).astype(jnp.bfloat16)
        value_out[rows_of, :] = (back * key_ref[rows_of, :].astype(jnp.float32)).astype(jnp.bfloat16)


def direct_body(query_act, key_act, value_act, out_grad, filters):
    tokens, chans = query_act.shape
    n = lax.axis_size("ctx")
    all_groups, taps_here = filters.shape
    groups = all_groups // n
    seq_len = tokens * n
    blocks = seq_len // BLOCK
    rows = blocks * GROUP_CH
    rows_here = rows // n
    anywhere = pl.BlockSpec(memory_space=pl.ANY)
    dma = pltpu.SemaphoreType.DMA
    macs = groups * 3 * (rows + GROUP_CH) // 2 * blocks * BLOCK * BLOCK
    returned, fgrad = pl.pallas_call(
        functools.partial(conv_kernel, n, 1.0 / math.sqrt(seq_len)),
        out_shape=(
            jax.ShapeDtypeStruct((all_groups, 2, rows_here, BLOCK), jnp.bfloat16),
            jax.ShapeDtypeStruct((all_groups, taps_here), jnp.float32),
        ),
        in_specs=[anywhere] * 5,
        out_specs=(anywhere, anywhere),
        scratch_shapes=[
            pltpu.VMEM((4, n, tokens, chans // n), jnp.bfloat16),
            pltpu.VMEM((all_groups, 2, rows_here, BLOCK), jnp.bfloat16),
            pltpu.VMEM((groups, 2, rows, BLOCK), jnp.bfloat16),
            pltpu.VMEM((groups, 2, rows, BLOCK), jnp.bfloat16),
            pltpu.VMEM((n, groups, taps_here), jnp.float32),
            pltpu.VMEM((n, groups, taps_here), jnp.float32),
            pltpu.VMEM((groups, seq_len // LANES, LANES), jnp.float32),
            pltpu.VMEM((groups, seq_len // LANES, LANES), jnp.float32),
            pltpu.VMEM((BLOCK, seq_len), jnp.bfloat16),
            pltpu.VMEM((rows + LANES, BLOCK), jnp.bfloat16),
            pltpu.VMEM((rows, BLOCK), jnp.float32),
            pltpu.VMEM((rows, BLOCK), jnp.float32),
            dma((groups, n)),
            dma((groups, n)),
            dma((groups, n)),
            dma((groups, n)),
            dma((n,)),
            dma((n,)),
            dma((n,)),
            dma((n,)),
            dma((4,)),
            dma((4, n)),
        ],
        compiler_params=pltpu.CompilerParams(
            collective_id=0, has_side_effects=True, vmem_limit_bytes=56 * 1024 * 1024
        ),
        cost_estimate=pl.CostEstimate(flops=2 * macs, bytes_accessed=16 * tokens * chans, transcendentals=0),
    )(query_act, key_act, value_act, out_grad, filters)
    strip = pl.BlockSpec((tokens, LANES), lambda i: (0, i))
    side = jax.ShapeDtypeStruct((tokens, chans), jnp.bfloat16)
    fgrad_rows = pl.BlockSpec((LANES // GROUP_CH, taps_here), lambda i: (i, 0))
    return pl.pallas_call(
        finish_kernel,
        grid=(chans // LANES,),
        out_shape=(side, side, side, jax.ShapeDtypeStruct(fgrad.shape, fgrad.dtype)),
        in_specs=[
            strip,
            strip,
            strip,
            pl.BlockSpec((LANES // GROUP_CH, 2, rows_here, BLOCK), lambda i: (i, 0, 0, 0)),
            fgrad_rows,
        ],
        out_specs=(strip, strip, strip, fgrad_rows),
        compiler_params=pltpu.CompilerParams(vmem_limit_bytes=56 * 1024 * 1024),
        cost_estimate=pl.CostEstimate(
            flops=3 * tokens * chans, bytes_accessed=16 * tokens * chans, transcendentals=0
        ),
    )(key_act, value_act, out_grad, returned, fgrad)


def body(query_act, key_act, value_act, out_grad, filters):
    tokens, chans = query_act.shape
    n = lax.axis_size("ctx")
    groups = filters.shape[0] // n
    fits = (
        tokens % BLOCK == 0
        and chans % LANES == 0
        and filters.shape[1] % LANES == 0
        and groups % 8 == 0
        and tokens * n // BLOCK <= MAX_BLOCKS
    )
    if fits:
        return direct_body(query_act, key_act, value_act, out_grad, filters)
    return spectral_body(query_act, key_act, value_act, out_grad, filters)


def solution(mesh):
    return jax.shard_map(
        body,
        mesh=mesh,
        in_specs=(P("ctx", "tp"), P("ctx", "tp"), P("ctx", "tp"), P("ctx", "tp"), P("tp", "ctx")),
        out_specs=(P("ctx", "tp"), P("ctx", "tp"), P("ctx", "tp"), P("tp", "ctx")),
        check_vma=False,
    )
```

```python
import functools
import math

import jax
import jax.numpy as jnp
from jax import lax
from jax.experimental import pallas as pl
from jax.experimental.pallas import tpu as pltpu
from jax.sharding import PartitionSpec as P

GROUP_CH = 16


HIGH = lax.Precision.HIGHEST


def make_tables(outer_len, inner_len, full_len):
    half_rows = outer_len // 2
    freq_idx = lax.iota(jnp.int32, outer_len)[:, None]
    time_idx = lax.iota(jnp.int32, half_rows)[None, :]
    outer_angle = (freq_idx * time_idx % outer_len).astype(jnp.float32) * (
        2.0 * math.pi / outer_len
    )
    inner_idx = lax.iota(jnp.int32, inner_len)
    inner_angle = (inner_idx[:, None] * inner_idx[None, :] % inner_len).astype(jnp.float32) * (
        2.0 * math.pi / inner_len
    )
    inner_cos = jnp.cos(inner_angle)
    inner_sin = jnp.sin(inner_angle)
    forward_mat = jnp.concatenate(
        [jnp.concatenate([inner_cos, -inner_sin], 1), jnp.concatenate([inner_sin, inner_cos], 1)], 0
    )
    inverse_mat = jnp.concatenate(
        [jnp.concatenate([inner_cos, inner_sin], 1), jnp.concatenate([-inner_sin, inner_cos], 1)], 0
    )
    twist_angle = (freq_idx * inner_idx[None, :] % full_len).astype(jnp.float32) * (
        2.0 * math.pi / full_len
    )
    return (
        jnp.cos(outer_angle),
        jnp.sin(outer_angle),
        forward_mat,
        inverse_mat,
        jnp.cos(twist_angle),
        jnp.sin(twist_angle),
    )


def transform(signal, tables):
    outer_cos, outer_sin, forward_mat, inverse_mat, twist_cos, twist_sin = tables
    outer_len, half_rows = outer_cos.shape
    inner_len = twist_cos.shape[1]
    count = signal.shape[0]
    folded = signal.reshape(count, half_rows, inner_len)
    first_re = jnp.einsum("ka,cab->ckb", outer_cos, folded, precision=HIGH)
    first_im = -jnp.einsum("ka,cab->ckb", outer_sin, folded, precision=HIGH)
    turned_re = first_re * twist_cos + first_im * twist_sin
    turned_im = first_im * twist_cos - first_re * twist_sin
    joined = jnp.concatenate([turned_re, turned_im], -1).reshape(count * outer_len, 2 * inner_len)
    spectrum = jnp.dot(joined, forward_mat, precision=HIGH, preferred_element_type=jnp.float32)
    spectrum = spectrum.reshape(count, outer_len, 2 * inner_len)
    return (spectrum[..., :inner_len], spectrum[..., inner_len:])


def untransform(real_part, imag_part, tables):
    outer_cos, outer_sin, forward_mat, inverse_mat, twist_cos, twist_sin = tables
    outer_len, half_rows = outer_cos.shape
    inner_len = twist_cos.shape[1]
    count = real_part.shape[0]
    joined = jnp.concatenate([real_part, imag_part], -1).reshape(count * outer_len, 2 * inner_len)
    mixed = jnp.dot(joined, inverse_mat, precision=HIGH, preferred_element_type=jnp.float32)
    mixed = mixed.reshape(count, outer_len, 2 * inner_len)
    mixed_re = mixed[..., :inner_len]
    mixed_im = mixed[..., inner_len:]
    turned_re = mixed_re * twist_cos - mixed_im * twist_sin
    turned_im = mixed_re * twist_sin + mixed_im * twist_cos
    signal = jnp.einsum("ka,ckb->cab", outer_cos, turned_re, precision=HIGH) - jnp.einsum(
        "ka,ckb->cab", outer_sin, turned_im, precision=HIGH
    )
    return signal.reshape(count, half_rows * inner_len) / (2.0 * half_rows * inner_len)


def convolve(kv_prod, gated, spread, tables, filter_scale):
    channels = kv_prod.shape[0]
    groups_here = spread.shape[0]
    outer_len = tables[0].shape[0]
    inner_len = tables[4].shape[1]
    filt_re, filt_im = transform(spread, tables)
    filt_re = (filt_re * filter_scale)[:, None]
    filt_im = (filt_im * filter_scale)[:, None]
    both_re, both_im = transform(jnp.concatenate([kv_prod, gated], 0).astype(jnp.float32), tables)
    grouped = (groups_here, GROUP_CH, outer_len, inner_len)
    kv_re = both_re[:channels].reshape(grouped)
    kv_im = both_im[:channels].reshape(grouped)
    gated_re = both_re[channels:].reshape(grouped)
    gated_im = both_im[channels:].reshape(grouped)
    out_re = filt_re * kv_re - filt_im * kv_im
    out_im = filt_re * kv_im + filt_im * kv_re
    back_re = filt_re * gated_re + filt_im * gated_im
    back_im = filt_re * gated_im - filt_im * gated_re
    cross_re = jnp.sum(kv_re * gated_re + kv_im * gated_im, 1)
    cross_im = jnp.sum(kv_re * gated_im - kv_im * gated_re, 1)
    flat = (channels, outer_len, inner_len)
    stacked_re = jnp.concatenate([out_re.reshape(flat), back_re.reshape(flat), cross_re], 0)
    stacked_im = jnp.concatenate([out_im.reshape(flat), back_im.reshape(flat), cross_im], 0)
    signals = untransform(stacked_re, stacked_im, tables)
    conv_out = signals[:channels].astype(jnp.bfloat16)
    conv_grad = signals[channels : 2 * channels].astype(jnp.bfloat16)
    filt_grad = signals[2 * channels :] * filter_scale
    return (conv_out, conv_grad, filt_grad)


def product(first, second):
    return (first.astype(jnp.float32) * second.astype(jnp.float32)).astype(jnp.bfloat16)


def spectral_body(query_act, key_act, value_act, out_grad, filters):
    tokens = query_act.shape[0]
    ctx_size = lax.axis_size("ctx")
    seq_len = tokens * ctx_size
    full_len = 2 * seq_len
    inner_len = math.gcd(full_len, 1 << full_len.bit_length() // 2)
    outer_len = full_len // inner_len
    tables = make_tables(outer_len, inner_len, full_len)
    filter_scale = 1.0 / math.sqrt(seq_len)
    spread = lax.all_to_all(filters, "ctx", split_axis=0, concat_axis=1, tiled=True)
    kv_local = product(key_act, value_act).T
    gated_local = product(out_grad, query_act).T
    kv_prod, gated = (
        lax.all_to_all(kv_local, "ctx", split_axis=0, concat_axis=1, tiled=True),
        lax.all_to_all(gated_local, "ctx", split_axis=0, concat_axis=1, tiled=True),
    )
    conv_out, conv_grad, filt_grad = convolve(kv_prod, gated, spread, tables, filter_scale)
    filter_grad = lax.all_to_all(filt_grad, "ctx", split_axis=1, concat_axis=0, tiled=True)
    returned = (
        lax.all_to_all(conv_out, "ctx", split_axis=1, concat_axis=0, tiled=True),
        lax.all_to_all(conv_grad, "ctx", split_axis=1, concat_axis=0, tiled=True),
    )
    conv_local = returned[0].T
    grad_local = returned[1].T
    query_grad = product(out_grad, conv_local)
    key_grad = product(grad_local, value_act)
    value_grad = product(grad_local, key_act)
    return (query_grad, key_grad, value_grad, filter_grad)


LANES = 128
BLOCK = 2 * LANES
MAX_BLOCKS = 16
EARLY = 2
MESH = pl.DeviceIdType.MESH


def dot(left, right, contract):
    return lax.dot_general(left, right, (contract, ((), ())), preferred_element_type=jnp.float32)


def diagonal_sums(tile):
    rows = LANES
    while rows > 8:
        rows //= 2
        tile = tile[:rows] + pltpu.roll(tile[rows:], LANES - rows, 1)
    row = lax.broadcasted_iota(jnp.int32, tile.shape, 0)
    for step in (4, 2, 1):
        tile = jnp.where(row // step % 2 == 1, pltpu.roll(tile, LANES - step, 1), tile)
    return jnp.sum(tile, axis=0, keepdims=True)


def conv_kernel(
    n,
    scale,
    query_ref,
    key_ref,
    value_ref,
    grad_ref,
    filt_ref,
    ret_ref,
    fgrad_ref,
    held,
    outbox,
    inbox,
    results,
    taps,
    tap_grads,
    tap_rows,
    grad_rows,
    toeplitz,
    padded,
    conv_acc,
    back_acc,
    fwd_send,
    fwd_recv,
    ret_send,
    ret_recv,
    tap_send,
    tap_recv,
    fg_send,
    fg_recv,
    local_sems,
    load_sems,
):
    me = lax.axis_index("ctx")
    tokens, chans = query_ref.shape
    parts = tokens // BLOCK
    rows_here = parts * GROUP_CH
    groups = inbox.shape[0]
    rows = inbox.shape[2]
    blocks = rows // GROUP_CH
    lanes_here = chans // n

    barrier = pltpu.get_barrier_semaphore()
    peers = [lax.rem(me + step, n) for step in range(1, n)]
    for peer in peers:
        pl.semaphore_signal(barrier, inc=1, device_id={"ctx": peer}, device_id_type=MESH)

    arrays = (key_ref, value_ref, grad_ref, query_ref)

    def load(which, dest):
        strip = pl.ds(pl.multiple_of(dest * lanes_here, lanes_here), lanes_here)
        return pltpu.make_async_copy(
            arrays[which].at[:, strip], held.at[which, dest], load_sems.at[which, dest]
        )

    for step in range(1, n + 1):
        for which in range(4):
            load(which, lax.rem(me + step, n)).start()

    def fill(dest):
        for which in range(4):
            load(which, dest).wait()
        for strip in range(lanes_here // LANES):
            lane = pl.ds(strip * LANES, LANES)
            first = dest * groups + strip * (LANES // GROUP_CH)
            for part in range(parts):
                rows_of = pl.ds(part * BLOCK, BLOCK)
                for which in range(2):
                    one = held[2 * which, dest, rows_of, lane].astype(jnp.float32)
                    two = held[2 * which + 1, dest, rows_of, lane].astype(jnp.float32)
                    turned = (one * two).astype(jnp.bfloat16).T
                    outbox[
                        pl.ds(first, LANES // GROUP_CH), which, pl.ds(part * GROUP_CH, GROUP_CH), :
                    ] = turned.reshape(LANES // GROUP_CH, GROUP_CH, BLOCK)

    def tap_copy(peer):
        return pltpu.make_async_remote_copy(
            src_ref=filt_ref.at[pl.ds(pl.multiple_of(peer * groups, groups), groups), :],
            dst_ref=taps.at[me],
            send_sem=tap_send.at[peer],
            recv_sem=tap_recv.at[me],
            device_id={"ctx": peer},
            device_id_type=MESH,
        )

    def fwd_copy(group, peer):
        return pltpu.make_async_remote_copy(
            src_ref=outbox.at[peer * groups + group],
            dst_ref=inbox.at[group, :, pl.ds(pl.multiple_of(me * rows_here, rows_here), rows_here), :],
            send_sem=fwd_send.at[group, peer],
            recv_sem=fwd_recv.at[group, me],
            device_id={"ctx": peer},
            device_id_type=MESH,
        )

    def fwd_arrival(group, peer):
        return pltpu.make_async_remote_copy(
            src_ref=outbox.at[peer * groups + group],
            dst_ref=inbox.at[group, :, pl.ds(pl.multiple_of(peer * rows_here, rows_here), rows_here), :],
            send_sem=fwd_send.at[group, peer],
            recv_sem=fwd_recv.at[group, peer],
            device_id={"ctx": peer},
            device_id_type=MESH,
        )

    def ret_copy(group, peer):
        return pltpu.make_async_remote_copy(
            src_ref=results.at[group, :, pl.ds(pl.multiple_of(peer * rows_here, rows_here), rows_here), :],
            dst_ref=ret_ref.at[me * groups + group],
            send_sem=ret_send.at[group, peer],
            recv_sem=ret_recv.at[group, me],
            device_id={"ctx": peer},
            device_id_type=MESH,
        )

    def ret_arrival(group, peer):
        return pltpu.make_async_remote_copy(
            src_ref=results.at[group, :, pl.ds(pl.multiple_of(peer * rows_here, rows_here), rows_here), :],
            dst_ref=ret_ref.at[peer * groups + group],
            send_sem=ret_send.at[group, peer],
            recv_sem=ret_recv.at[group, peer],
            device_id={"ctx": peer},
            device_id_type=MESH,
        )

    def fg_copy(peer):
        return pltpu.make_async_remote_copy(
            src_ref=tap_grads.at[peer],
            dst_ref=fgrad_ref.at[pl.ds(pl.multiple_of(me * groups, groups), groups), :],
            send_sem=fg_send.at[peer],
            recv_sem=fg_recv.at[me],
            device_id={"ctx": peer},
            device_id_type=MESH,
        )

    def fg_arrival(peer):
        return pltpu.make_async_remote_copy(
            src_ref=tap_grads.at[peer],
            dst_ref=fgrad_ref.at[pl.ds(pl.multiple_of(peer * groups, groups), groups), :],
            send_sem=fg_send.at[peer],
            recv_sem=fg_recv.at[peer],
            device_id={"ctx": peer},
            device_id_type=MESH,
        )

    def tap_arrival(peer):
        return pltpu.make_async_remote_copy(
            src_ref=filt_ref.at[pl.ds(pl.multiple_of(peer * groups, groups), groups), :],
            dst_ref=taps.at[peer],
            send_sem=tap_send.at[peer],
            recv_sem=tap_recv.at[peer],
            device_id={"ctx": peer},
            device_id_type=MESH,
        )

    pl.semaphore_wait(barrier, n - 1)
    for peer in peers:
        tap_copy(peer).start()

    def fill_and_send(step, carry):
        dest = lax.rem(me + step, n)
        fill(dest)
        for group in range(EARLY):
            fwd_copy(group, dest).start()
        return carry

    lax.fori_loop(1, n, fill_and_send, 0)

    def send_group(group, carry):
        for peer in peers:
            fwd_copy(group, peer).start()
        return carry

    lax.fori_loop(EARLY, groups, send_group, 0)
    fill(me)
    own_rows = pl.ds(pl.multiple_of(me * rows_here, rows_here), rows_here)
    own_groups = pl.ds(pl.multiple_of(me * groups, groups), groups)
    own_taps = pltpu.make_async_copy(filt_ref.at[own_groups, :], taps.at[me], local_sems.at[0])
    own_in = pltpu.make_async_copy(outbox.at[own_groups], inbox.at[:, :, own_rows, :], local_sems.at[1])
    own_taps.start()
    own_in.start()

    padded[pl.ds(rows, LANES), :] = jnp.zeros((LANES, BLOCK), jnp.bfloat16)
    toeplitz[pl.ds(LANES, LANES), pl.ds(0, LANES)] = jnp.zeros((LANES, LANES), jnp.bfloat16)
    own_taps.wait()
    own_in.wait()
    for peer in peers:
        tap_arrival(peer).wait_recv()

    tiles = rows * BLOCK // GROUP_CH // LANES
    per_dev = tiles // n
    for group in range(groups):
        for tile in range(tiles):
            tap_rows[group, pl.ds(tile, 1), :] = (
                taps[tile // per_dev, pl.ds(group, 1), pl.ds(tile % per_dev * LANES, LANES)] * scale
            )
    row_idx = lax.broadcasted_iota(jnp.int32, (LANES, LANES), 0)
    lane_idx = lax.broadcasted_iota(jnp.int32, (LANES, LANES), 1)
    upper = lane_idx >= row_idx

    def one_group(group, carry):
        before = jnp.zeros((LANES, LANES), jnp.float32)
        for tile in range(tiles):
            line = tap_rows[group, pl.ds(tile, 1), :]
            now = pltpu.roll(jnp.broadcast_to(line, (LANES, LANES)), 0, 1, stride=1, stride_axis=0)
            both = jnp.where(upper, now, before).astype(jnp.bfloat16)
            toeplitz[pl.ds(0, LANES), pl.ds(tile * LANES, LANES)] = both
            if tile + 1 < tiles:
                toeplitz[pl.ds(LANES, LANES), pl.ds((tile + 1) * LANES, LANES)] = both
            before = now
        for peer in peers:
            fwd_arrival(group, peer).wait_recv()
        padded[pl.ds(0, rows), :] = inbox[group, 1]
        turned = inbox[group, 0].T
        even_after = jnp.zeros((LANES, LANES), jnp.float32)
        carried = jnp.zeros((LANES, LANES), jnp.float32)
        conv_acc[...] = jnp.zeros(conv_acc.shape, jnp.float32)
        back_acc[...] = jnp.zeros(back_acc.shape, jnp.float32)
        for gap in reversed(range(blocks)):
            skip = gap * GROUP_CH
            count = rows - skip
            block_taps = toeplitz[:, pl.ds(gap * BLOCK, BLOCK)]
            conv_acc[pl.ds(skip, count), :] += dot(
                inbox[group, 0, pl.ds(0, count), :], block_taps, ((1,), (0,))
            )
            back_acc[pl.ds(0, count), :] += dot(
                padded[pl.ds(skip, count), :], block_taps, ((1,), (1,))
            )
            depth = -(-count // LANES) * LANES
            cross = dot(turned[:, :depth], padded[pl.ds(skip, depth), :], ((1,), (0,)))
            odd = cross[:LANES, LANES:] + carried
            even = cross[:LANES, :LANES] + cross[LANES:, LANES:]
            carried = cross[LANES:, :LANES]
            for tile, picked in (
                (2 * gap + 1, jnp.where(upper, odd, even_after)),
                (2 * gap, jnp.where(upper, even, odd)),
            ):
                grad_rows[group, pl.ds(tile, 1), :] = diagonal_sums(picked) * scale
            even_after = even
        results[group, 0] = conv_acc[...].astype(jnp.bfloat16)
        results[group, 1] = back_acc[...].astype(jnp.bfloat16)
        for peer in peers:
            ret_copy(group, peer).start()
        return carry

    lax.fori_loop(0, groups, one_group, 0)
    for group in range(groups):
        for tile in range(tiles):
            tap_grads[tile // per_dev, pl.ds(group, 1), pl.ds(tile % per_dev * LANES, LANES)] = (
                grad_rows[group, pl.ds(tile, 1), :]
            )
    for peer in peers:
        fg_copy(peer).start()
    own_ret = pltpu.make_async_copy(results.at[:, :, own_rows, :], ret_ref.at[own_groups], local_sems.at[2])
    own_fg = pltpu.make_async_copy(tap_grads.at[me], fgrad_ref.at[own_groups, :], local_sems.at[3])
    own_ret.start()
    own_fg.start()

    def finish_group(group, carry):
        for peer in peers:
            fwd_copy(group, peer).wait_send()
            ret_copy(group, peer).wait_send()
            ret_arrival(group, peer).wait_recv()
        return carry

    lax.fori_loop(0, groups, finish_group, 0)
    for peer in peers:
        tap_copy(peer).wait_send()
        fg_copy(peer).wait_send()
        fg_arrival(peer).wait_recv()
    own_ret.wait()
    own_fg.wait()


def finish_kernel(
    key_ref, value_ref, grad_ref, ret_ref, fgrad_ref, query_out, key_out, value_out, fgrad_out
):
    fgrad_out[...] = fgrad_ref[...]
    per_strip = LANES // GROUP_CH
    for strip in range(key_ref.shape[1] // LANES):
        lane = pl.ds(strip * LANES, LANES)
        turned = []
        for which in range(2):
            piece = ret_ref[pl.ds(strip * per_strip, per_strip), which, :, :]
            turned.append(piece.reshape(LANES, LANES).T.astype(jnp.float32))
        conv, back = turned
        query_out[:, lane] = (grad_ref[:, lane].astype(jnp.float32) * conv).astype(jnp.bfloat16)
        key_out[:, lane] = (back * value_ref[:, lane].astype(jnp.float32)).astype(jnp.bfloat16)
        value_out[:, lane] = (back * key_ref[:, lane].astype(jnp.float32)).astype(jnp.bfloat16)


def direct_body(query_act, key_act, value_act, out_grad, filters):
    tokens, chans = query_act.shape
    n = lax.axis_size("ctx")
    all_groups, taps_here = filters.shape
    groups = all_groups // n
    seq_len = tokens * n
    blocks = seq_len // BLOCK
    rows = blocks * GROUP_CH
    rows_here = rows // n
    anywhere = pl.BlockSpec(memory_space=pl.ANY)
    dma = pltpu.SemaphoreType.DMA
    macs = groups * 3 * (rows + GROUP_CH) // 2 * blocks * BLOCK * BLOCK
    returned, fgrad = pl.pallas_call(
        functools.partial(conv_kernel, n, 1.0 / math.sqrt(seq_len)),
        out_shape=(
            jax.ShapeDtypeStruct((all_groups, 2, rows_here, BLOCK), jnp.bfloat16),
            jax.ShapeDtypeStruct((all_groups, taps_here), jnp.float32),
        ),
        in_specs=[anywhere] * 5,
        out_specs=(anywhere, anywhere),
        scratch_shapes=[
            pltpu.VMEM((4, n, tokens, chans // n), jnp.bfloat16),
            pltpu.VMEM((all_groups, 2, rows_here, BLOCK), jnp.bfloat16),
            pltpu.VMEM((groups, 2, rows, BLOCK), jnp.bfloat16),
            pltpu.VMEM((groups, 2, rows, BLOCK), jnp.bfloat16),
            pltpu.VMEM((n, groups, taps_here), jnp.float32),
            pltpu.VMEM((n, groups, taps_here), jnp.float32),
            pltpu.VMEM((groups, seq_len // LANES, LANES), jnp.float32),
            pltpu.VMEM((groups, seq_len // LANES, LANES), jnp.float32),
            pltpu.VMEM((BLOCK, seq_len), jnp.bfloat16),
            pltpu.VMEM((rows + LANES, BLOCK), jnp.bfloat16),
            pltpu.VMEM((rows, BLOCK), jnp.float32),
            pltpu.VMEM((rows, BLOCK), jnp.float32),
            dma((groups, n)),
            dma((groups, n)),
            dma((groups, n)),
            dma((groups, n)),
            dma((n,)),
            dma((n,)),
            dma((n,)),
            dma((n,)),
            dma((4,)),
            dma((4, n)),
        ],
        compiler_params=pltpu.CompilerParams(
            collective_id=0, has_side_effects=True, vmem_limit_bytes=56 * 1024 * 1024
        ),
        cost_estimate=pl.CostEstimate(flops=2 * macs, bytes_accessed=16 * tokens * chans, transcendentals=0),
    )(query_act, key_act, value_act, out_grad, filters)
    steps = tokens // LANES
    halves = BLOCK // LANES
    strip = pl.BlockSpec((LANES, chans), lambda i: (i, 0))
    side = jax.ShapeDtypeStruct((tokens, chans), jnp.bfloat16)
    fgrad_rows = pl.BlockSpec((all_groups // steps, taps_here), lambda i: (i, 0))
    return pl.pallas_call(
        finish_kernel,
        grid=(steps,),
        out_shape=(side, side, side, jax.ShapeDtypeStruct(fgrad.shape, fgrad.dtype)),
        in_specs=[
            strip,
            strip,
            strip,
            pl.BlockSpec((all_groups, 2, GROUP_CH, LANES), lambda i: (0, 0, i // halves, i % halves)),
            fgrad_rows,
        ],
        out_specs=(strip, strip, strip, fgrad_rows),
        compiler_params=pltpu.CompilerParams(vmem_limit_bytes=56 * 1024 * 1024),
        cost_estimate=pl.CostEstimate(
            flops=3 * tokens * chans, bytes_accessed=16 * tokens * chans, transcendentals=0
        ),
    )(key_act, value_act, out_grad, returned, fgrad)


def body(query_act, key_act, value_act, out_grad, filters):
    tokens, chans = query_act.shape
    n = lax.axis_size("ctx")
    groups = filters.shape[0] // n
    fits = (
        tokens % BLOCK == 0
        and chans % LANES == 0
        and filters.shape[1] % LANES == 0
        and groups % 8 == 0
        and filters.shape[0] % (tokens // LANES * 8) == 0
        and tokens * n // BLOCK <= MAX_BLOCKS
    )
    if fits:
        return direct_body(query_act, key_act, value_act, out_grad, filters)
    return spectral_body(query_act, key_act, value_act, out_grad, filters)


def solution(mesh):
    return jax.shard_map(
        body,
        mesh=mesh,
        in_specs=(P("ctx", "tp"), P("ctx", "tp"), P("ctx", "tp"), P("ctx", "tp"), P("tp", "ctx")),
        out_specs=(P("ctx", "tp"), P("ctx", "tp"), P("ctx", "tp"), P("tp", "ctx")),
        check_vma=False,
    )
```
